256 devices in a mesh: shard: 16 (over y_lo, z), layer: 16 (over x, y_hi, core).
Axes of the slice: x: 4, y: 4 (y_hi: 2, y_lo: 2; y = y_hi * 2 + y_lo), z: 8, core: 2. Of those that a mesh axis runs over, the one named last changes fastest.
Arguments:
- grad: bfloat16 [16, 4608, 1024], P('layer', None, 'shard'), may hold values from -6 to 6
- momentum: float32 [16, 4608, 1024], P('layer', None, 'shard'), may hold values from -18 to 18
- second: float32 [16, 4608, 1024], P('layer', 'shard'), may hold values from 0.1 to 4
- left_slots: bfloat16 [16, 16, 1152, 1152], P('layer', 'shard'), may hold values from -0.1875 to 0.1875
- right_slots: bfloat16 [16, 16, 1024, 1024], P('layer', 'shard'), may hold values from -0.1875 to 0.1875
- owners: int32 [16, 16], P('layer'), may hold values from 0 to 15, each once within a row
Outputs:
- momentum_out: float32 [16, 4608, 1024], P('layer', None, 'shard')
- second_out: float32 [16, 4608, 1024], P('layer', 'shard')
- direction: bfloat16 [16, 4608, 1024], P('layer', None, 'shard')
The draws below stay inside these ranges and needn't reach their ends.
Inputs may be any that keep to these rules, and one draw needn't show every extreme that they name: Each row of owners names every slot 0 to 15 once; entries 0 to 4 name the slots of the basis blocks, the rest are unused.
All inputs are finite; a program needn't handle non-finite values.
Results may differ from the reference program's by a relative error of at most 0.0061.
Values may be sent and summed in bfloat16 or wider, within the bound.
No kernel may reach another device: no remote copies, remote signals or barrier semaphores. Data moves between devices by JAX's collectives and lax.ppermute only.
A program may use at most 128 MiB of HBM per device.

```python
import math
import jax
import jax.numpy as jnp
from jax import lax

R = 4608
C = 1024
BLK = 1152
LAYERS = 16
N_SHARD = 16


def draw_momentum(key, part):
    key = jax.random.fold_in(key, 7)
    layer_pos = jnp.arange(LAYERS, dtype=jnp.float32) / max(LAYERS - 1, 1)
    column_pos = jnp.arange(C, dtype=jnp.float32) / max(C - 1, 1)
    layer_scale = 0.5 * jnp.power(3.0, layer_pos)
    column_scale = jnp.power(3.0, column_pos)
    base = jnp.clip(jax.random.normal(key, (LAYERS, R, C), jnp.float32), -4.0, 4.0)
    return base * layer_scale[:, None, None] * column_scale[None, None, :]


def block_levels(own_key, shape, shards, smallest, high):
    gain = 1.0
    for position, shards_of in shards:
        steps = jax.random.uniform(jax.random.fold_in(jax.random.fold_in(own_key, 6), position), (shards_of,), jnp.float32, smallest / len(shards), high / len(shards))
        gain = gain * jnp.repeat(jnp.exp(steps), shape[position] // shards_of).reshape((-1,) + (1,) * (len(shape) - 1 - position))
    return gain


def noise(own_key, shape, scale, bound, cuts=(), kind=jnp.bfloat16):
    array = jax.random.normal(own_key, shape, jnp.float32) * scale
    if len(cuts) > 0:
        array = block_levels(own_key, shape, cuts, -0.22, 0.18) * array
    return jnp.clip(array, min=-bound, max=bound).astype(kind)


def setup_inputs(seed: int = 0) -> dict:
    key_list = jax.random.split(jax.random.key(seed), 7)
    grad = noise(key_list[0], (LAYERS, R, C), 1.0, 6.0, ((0, 16), (2, 16)))
    momentum = draw_momentum(jax.random.fold_in(key_list[6], 71), 0)
    second = jnp.clip(jnp.exp(math.log(4.0) - 3.6888794 * jax.random.uniform(key_list[2], (LAYERS, R, C), jnp.float32) ** block_levels(key_list[2], (LAYERS, R, C), ((0, 16), (1, 16)), -0.2, 0.2)), 0.1, 4.0)
    left_slots = noise(key_list[3], (LAYERS, N_SHARD, BLK, BLK), BLK ** -0.5, 0.1875, ((0, 16), (1, 16)))
    right_slots = noise(key_list[4], (LAYERS, N_SHARD, C, C), C ** -0.5, 0.1875, ((0, 16), (1, 16)))
    owners = jax.vmap(lambda own: jax.random.permutation(own, N_SHARD))(jax.random.split(key_list[5], LAYERS)).reshape((LAYERS, N_SHARD)).astype(jnp.int32)
    return dict(grad=grad, momentum=momentum, second=second, left_slots=left_slots, right_slots=right_slots, owners=owners)


first_decay = 0.9
second_decay = 0.95
guard_eps = 1e-08
clip_limit = 0.2

def left_rotate(blocks, values, pattern):
    count = blocks.shape[0]
    shaped = values.astype(jnp.float32).reshape(count, blocks.shape[1], values.shape[1])
    out = jnp.einsum(pattern, blocks.astype(jnp.float32), shaped)
    return out.reshape(values.shape)

def one_matrix(items):
    grad_one, moment_one, second_one, left_one, right_one, owner_one = items
    count = R // BLK
    blocks = left_one[owner_one[:count]]
    right = right_one[owner_one[count]]
    moment_new = first_decay * moment_one + (1.0 - first_decay) * grad_one.astype(jnp.float32)
    moment_half = moment_new.astype(jnp.bfloat16)
    grad_left = left_rotate(blocks, grad_one, 'bkr,bkn->brn').astype(jnp.bfloat16)
    moment_left = left_rotate(blocks, moment_half, 'bkr,bkn->brn').astype(jnp.bfloat16)
    grad_rot = jnp.dot(grad_left, right, preferred_element_type=jnp.float32)
    moment_rot = jnp.dot(moment_left, right, preferred_element_type=jnp.float32)
    second_new = second_decay * second_one + (1.0 - second_decay) * grad_rot * grad_rot
    scaled = (moment_rot / (jnp.sqrt(second_new) + guard_eps)).astype(jnp.bfloat16)
    back = jnp.dot(scaled, right.T, preferred_element_type=jnp.float32).astype(jnp.bfloat16)
    raw = left_rotate(blocks, back, 'brk,bkn->brn')
    return (moment_new, second_new, raw)

def reference(grad, momentum, second, left_slots, right_slots, owners):
    moment_new, second_new, raw = lax.map(one_matrix, (grad, momentum, second, left_slots, right_slots, owners))
    total = jnp.sum(raw * raw)
    mean_square = total / (LAYERS * R * C)
    factor = jnp.minimum(1.0, clip_limit / jnp.sqrt(mean_square + 1e-06))
    return (moment_new, second_new, (factor * raw).astype(jnp.bfloat16))
```

```python
import jax
import jax.numpy as jnp
from jax import lax
from jax.sharding import PartitionSpec as P

BLK = 1152
RING = 8
SIDES = 2

first_decay = 0.9
second_decay = 0.95
guard_eps = 1e-08
clip_limit = 0.2


def rings():
    return [[y * RING + z for z in range(RING)] for y in range(SIDES)]


def ring_shift(value, step):
    pairs = [(y * RING + z, y * RING + (z + step) % RING) for y in range(SIDES) for z in range(RING)]
    return lax.ppermute(value, "shard", pairs)


def cross(value):
    return lax.ppermute(value, "shard", [(s, (s + RING) % (RING * SIDES)) for s in range(RING * SIDES)])


def ring_all_to_all(value):
    return lax.all_to_all(value, "shard", 0, 0, axis_index_groups=rings())


def ring_gather(chunk, z, last_forward):
    rows = chunk.shape[0]
    whole = jnp.zeros((RING * rows,) + chunk.shape[1:], chunk.dtype)

    def put(whole, piece, place):
        return lax.dynamic_update_slice(whole, piece, (((place + RING) % RING) * rows, 0))

    whole = put(whole, chunk, z)
    forward = backward = chunk
    for step in range(1, RING // 2):
        forward = ring_shift(forward, 1)
        backward = ring_shift(backward, -1)
        whole = put(whole, forward, z - step)
        whole = put(whole, backward, z + step)
    if last_forward:
        far = ring_shift(forward, 1)
    else:
        far = ring_shift(backward, -1)
    return put(whole, far, z + RING // 2)


def total_over(value, axis):
    tile = jnp.full((lax.axis_size(axis), 8, 128), value)
    return jnp.sum(lax.all_to_all(tile, axis, 0, 0)[:, 0, 0])


def body(grad, momentum, second, left_slots, right_slots, owners):
    me = lax.axis_index("shard")
    y = me // RING
    z = me % RING
    rows_all = grad.shape[1]
    cols = grad.shape[2]
    half = rows_all // SIDES
    row_part = rows_all // (RING * SIDES)
    count = half // BLK
    width = right_slots.shape[-1]
    piece = BLK // RING
    own = owners[0]
    own_y = own // RING
    own_z = own % RING
    first = y == 0

    left = left_slots[0, 0].reshape(RING, piece, BLK)
    right = right_slots[0, 0].reshape(SIDES, RING, cols, width).transpose(1, 0, 2, 3)
    right = right.reshape(RING, SIDES * cols, width)
    right = jnp.pad(right, ((0, 0), (0, piece - SIDES * cols), (0, BLK - width)))
    item = jnp.where(own[SIDES * count] == me, right, left)
    eighths = ring_all_to_all(item)

    grad_t = grad[0].T
    moment_new = first_decay * momentum[0].T + (1.0 - first_decay) * grad_t.astype(jnp.float32)
    paired = jnp.stack([grad_t, moment_new.astype(jnp.bfloat16)])
    mine = lax.dynamic_slice_in_dim(paired, y * half, half, 2)
    other = cross(lax.dynamic_slice_in_dim(paired, (1 - y) * half, half, 2))
    both = jnp.where(
        first, jnp.concatenate([mine, other], 1), jnp.concatenate([other, mine], 1)
    ).reshape(2 * SIDES * cols, half)

    def pick(block):
        return lax.dynamic_index_in_dim(eighths, own_z[block], 0, keepdims=False)

    keep = jnp.stack([pick(y * count + i) for i in range(count)])
    give = jnp.stack([pick((1 - y) * count + i) for i in range(count)])
    took = cross(give)
    chunk = [
        jnp.where(own_y[y * count + i] == y, keep[i], took[i]) for i in range(count)
    ]
    right_piece = pick(SIDES * count)[: SIDES * cols, :width].reshape(SIDES, cols, width)
    keep_right = lax.dynamic_index_in_dim(right_piece, y, 0, keepdims=False)
    took_right = cross(lax.dynamic_index_in_dim(right_piece, 1 - y, 0, keepdims=False))
    right_chunk = jnp.where(own_y[SIDES * count] == y, keep_right, took_right)

    right_half = ring_gather(right_chunk, z, True).reshape(RING, cols, width)
    right_other = cross(right_half)
    right_all = jnp.where(
        first,
        jnp.stack([right_half, right_other], 1),
        jnp.stack([right_other, right_half], 1),
    ).reshape(RING * SIDES * cols, width)
    blocks = [ring_gather(chunk[i], z, i % 2 == 0) for i in range(count)]

    rotated = jnp.stack(
        [
            lax.dot_general(
                blocks[i],
                both[:, i * BLK : (i + 1) * BLK],
                (((0,), (1,)), ((), ())),
                preferred_element_type=jnp.float32,
            ).astype(jnp.bfloat16)
            for i in range(count)
        ]
    )
    values = ring_all_to_all(rotated.reshape(RING, row_part, 2 * SIDES * cols))
    values = values.reshape(RING, row_part, 2, SIDES * cols).transpose(2, 1, 0, 3)
    flat = values.reshape(2 * row_part, width)
    turned = jnp.dot(flat, right_all, preferred_element_type=jnp.float32)
    grad_rot = turned[:row_part]
    moment_rot = turned[row_part:]
    second_new = second_decay * second[0] + (1.0 - second_decay) * grad_rot * grad_rot
    scaled = (moment_rot / (jnp.sqrt(second_new) + guard_eps)).astype(jnp.bfloat16)
    back = lax.dot_general(
        scaled, right_all, (((1,), (1,)), ((), ())), preferred_element_type=jnp.float32
    ).astype(jnp.bfloat16)
    returning = back.reshape(row_part, RING, SIDES * cols).transpose(1, 0, 2)
    values = ring_all_to_all(returning).reshape(count, BLK, SIDES * cols)
    raw = jnp.concatenate(
        [
            lax.dot_general(
                values[i], blocks[i], (((0,), (1,)), ((), ())), preferred_element_type=jnp.float32
            )
            for i in range(count)
        ],
        1,
    )
    local_total = jnp.sum(raw * raw)
    raw_mine = lax.dynamic_slice_in_dim(raw, y * cols, cols, 0)
    raw_other = cross(lax.dynamic_slice_in_dim(raw, (1 - y) * cols, cols, 0).astype(jnp.bfloat16))
    raw_other = raw_other.astype(jnp.float32)
    total = total_over(total_over(local_total, "shard"), "layer")
    cells = lax.axis_size("layer") * grad.shape[0] * rows_all * cols * RING * SIDES
    factor = jnp.minimum(1.0, clip_limit / jnp.sqrt(total / cells + 1e-06))
    direction = jnp.where(
        first,
        jnp.concatenate([raw_mine, raw_other], 1),
        jnp.concatenate([raw_other, raw_mine], 1),
    )
    direction = (factor * direction).astype(jnp.bfloat16)
    return (moment_new.T[None], second_new[None], direction.T[None])


def solution(mesh):
    placed = (
        P("layer", None, "shard"),
        P("layer", None, "shard"),
        P("layer", "shard", None),
        P("layer", "shard", None, None),
        P("layer", "shard", None, None),
        P("layer", None),
    )
    return jax.shard_map(
        body,
        mesh=mesh,
        in_specs=placed,
        out_specs=(P("layer", None, "shard"), P("layer", "shard", None), P("layer", None, "shard")),
        check_vma=False,
    )
```

```python
import jax
import jax.numpy as jnp
from jax import lax
from jax.experimental import pallas as pl
from jax.experimental.pallas import tpu as pltpu
from jax.sharding import PartitionSpec as P

BLK = 1152
RING = 8
SIDES = 2
TILE = 256

first_decay = 0.9
second_decay = 0.95
guard_eps = 1e-08
clip_limit = 0.2


def rings():
    return [[y * RING + z for z in range(RING)] for y in range(SIDES)]


def ring_shift(value, step):
    pairs = [(y * RING + z, y * RING + (z + step) % RING) for y in range(SIDES) for z in range(RING)]
    return lax.ppermute(value, "shard", pairs)


def cross(value):
    return lax.ppermute(value, "shard", [(s, (s + RING) % (RING * SIDES)) for s in range(RING * SIDES)])


def ring_all_to_all(value):
    return lax.all_to_all(value, "shard", 0, 0, axis_index_groups=rings())


def ring_gather(chunks, z):
    rows = chunks[0].shape[0]
    whole = jnp.zeros((len(chunks), RING * rows) + chunks[0].shape[1:], chunks[0].dtype)

    def put(whole, piece, i, place):
        return lax.dynamic_update_slice(whole, piece[None], (i, ((place + RING) % RING) * rows, 0))

    forward = list(chunks)
    backward = list(chunks)
    for i, chunk in enumerate(chunks):
        whole = put(whole, chunk, i, z)
    for step in range(1, RING // 2):
        for i in range(len(chunks)):
            forward[i] = ring_shift(forward[i], 1)
            backward[i] = ring_shift(backward[i], -1)
            whole = put(whole, forward[i], i, z - step)
            whole = put(whole, backward[i], i, z + step)
    for i in range(len(chunks)):
        far = ring_shift(forward[i], 1) if i % 2 == 0 else ring_shift(backward[i], -1)
        whole = put(whole, far, i, z + RING // 2)
    return whole


def cut_kernel(owners, left, right, *pieces):
    me = lax.axis_index("shard")
    z = lax.rem(me, RING)
    holds_right = owners[0, owners.shape[1] // 4] == me
    rows, lanes = right.shape[1:]

    @pl.when(holds_right)
    def _():
        for step, piece in enumerate(pieces):
            piece[:rows, :lanes] = right[lax.rem(z + step, RING)]

    @pl.when(jnp.logical_not(holds_right))
    def _():
        for step, piece in enumerate(pieces):
            piece[...] = left[lax.rem(z + step, RING)]


def cut_slot(owners, left, right):
    return pl.pallas_call(
        cut_kernel,
        out_shape=[jax.ShapeDtypeStruct(left.shape[1:], left.dtype)] * RING,
        in_specs=[
            pl.BlockSpec(memory_space=pltpu.SMEM),
            pl.BlockSpec(memory_space=pltpu.VMEM),
            pl.BlockSpec(memory_space=pltpu.VMEM),
        ],
        compiler_params=pltpu.CompilerParams(vmem_limit_bytes=24 * 1024 * 1024),
    )(owners, left, right)


def raw_kernel(values, blocks, mine, other, sums):
    y = lax.div(lax.axis_index("shard"), RING)
    cols = mine.shape[0]
    order = blocks.shape[1]
    step = order // 3
    total = jnp.zeros((1, 128), jnp.float32)
    for i in range(blocks.shape[0]):
        back = values[i].T
        for j in range(order // step):
            raw = lax.dot_general(
                back,
                blocks[i, j * step : (j + 1) * step, :],
                (((1,), (1,)), ((), ())),
                preferred_element_type=jnp.float32,
            )
            low = raw[:cols]
            high = raw[cols:]
            lanes = slice(i * order + j * step, i * order + (j + 1) * step)
            mine[:, lanes] = jnp.where(y == 0, low, high)
            other[:, lanes] = jnp.where(y == 0, high, low).astype(jnp.bfloat16)
            square = jnp.sum(raw * raw, 0, keepdims=True)
            for k in range(step // 128):
                total += square[:, k * 128 : (k + 1) * 128]
    sums[...] = jnp.broadcast_to(total, sums.shape)


def raw_stage(values, blocks, devices):
    count, order, pairs = values.shape
    shape = (pairs // SIDES, count * order)
    return pl.pallas_call(
        raw_kernel,
        out_shape=(
            jax.ShapeDtypeStruct(shape, jnp.float32),
            jax.ShapeDtypeStruct(shape, jnp.bfloat16),
            jax.ShapeDtypeStruct((devices, 128), jnp.float32),
        ),
        compiler_params=pltpu.CompilerParams(vmem_limit_bytes=24 * 1024 * 1024),
    )(values, blocks)


def right_kernel(values, right, second, second_out, out, scaled):
    rows = second.shape[0]
    pair = out.shape[2]
    places = values.shape[0]
    grad_left = jnp.concatenate([values[i, :, :pair] for i in range(places)], 1)
    moment_left = jnp.concatenate([values[i, :, pair:] for i in range(places)], 1)

    def turn(j, carry):
        lanes = pl.ds(pl.multiple_of(j * TILE, TILE), TILE)
        basis = right[:, lanes]
        grad_rot = jnp.dot(grad_left, basis, preferred_element_type=jnp.float32)
        moment_rot = jnp.dot(moment_left, basis, preferred_element_type=jnp.float32)
        second_new = second_decay * second[:, lanes] + (1.0 - second_decay) * grad_rot * grad_rot
        second_out[:, lanes] = second_new
        scaled[:, lanes] = (moment_rot / (jnp.sqrt(second_new) + guard_eps)).astype(jnp.bfloat16)
        return carry

    lax.fori_loop(0, second.shape[1] // TILE, turn, 0)

    def turn_back(j, carry):
        basis = right[pl.ds(pl.multiple_of(j * TILE, TILE), TILE), :]
        back = lax.dot_general(
            scaled[...], basis, (((1,), (1,)), ((), ())), preferred_element_type=jnp.float32
        ).astype(jnp.bfloat16)
        for i in range(TILE // pair):
            out[j * (TILE // pair) + i] = back[:, i * pair : (i + 1) * pair]
        return carry

    lax.fori_loop(0, right.shape[0] // TILE, turn_back, 0)


def right_stage(values, right, second):
    places, rows, pairs = values.shape
    return pl.pallas_call(
        right_kernel,
        out_shape=(
            jax.ShapeDtypeStruct(second.shape, jnp.float32),
            jax.ShapeDtypeStruct((places, rows, pairs // 2), jnp.bfloat16),
        ),
        scratch_shapes=[pltpu.VMEM(second.shape, jnp.bfloat16)],
        compiler_params=pltpu.CompilerParams(vmem_limit_bytes=24 * 1024 * 1024),
    )(values, right, second)


def body(grad, momentum, second, left_slots, right_slots, owners):
    me = lax.axis_index("shard")
    y = me // RING
    z = me % RING
    rows_all = grad.shape[1]
    cols = grad.shape[2]
    half = rows_all // SIDES
    row_part = rows_all // (RING * SIDES)
    count = half // BLK
    width = right_slots.shape[-1]
    piece = BLK // RING
    own = owners[0]
    own_y = own // RING
    own_z = own % RING
    first = y == 0

    pieces = cut_slot(
        owners,
        left_slots[0, 0].reshape(RING, piece, BLK),
        right_slots[0, 0].reshape(RING, SIDES * cols, width),
    )
    eighths = jnp.zeros((RING, piece, BLK), jnp.bfloat16)
    for step in (0, 4, 3, 5, 2, 6, 1, 7):
        part = pieces[step]
        if step:
            part = ring_shift(part, step)
        eighths = lax.dynamic_update_slice(eighths, part[None], ((z - step + RING) % RING, 0, 0))

    grad_t = grad[0].T
    moment_new = first_decay * momentum[0].T + (1.0 - first_decay) * grad_t.astype(jnp.float32)
    paired = jnp.stack([grad_t, moment_new.astype(jnp.bfloat16)])
    mine = lax.dynamic_slice_in_dim(paired, y * half, half, 2)
    other = cross(lax.dynamic_slice_in_dim(paired, (1 - y) * half, half, 2))
    eighths, other = lax.optimization_barrier((eighths, other))
    both = jnp.where(
        first, jnp.concatenate([mine, other], 1), jnp.concatenate([other, mine], 1)
    ).reshape(2 * SIDES * cols, half)
    both = jnp.stack([both[:, i * BLK : (i + 1) * BLK] for i in range(count)])

    def pick(block):
        return lax.dynamic_index_in_dim(eighths, own_z[block], 0, keepdims=False)

    side = width // SIDES
    keep_right = pick(SIDES * count)[: SIDES * cols, :width]
    give_right = lax.dynamic_slice_in_dim(keep_right, (1 - y) * side, side, 1)
    keep_right = lax.dynamic_slice_in_dim(keep_right, y * side, side, 1)
    took_right = cross(give_right)
    right_chunk = jnp.where(own_y[SIDES * count] == y, keep_right, took_right)
    took = [cross(pick((1 - y) * count + i)) for i in range(count)]
    chunk = [
        jnp.where(own_y[y * count + i] == y, pick(y * count + i), took[i]) for i in range(count)
    ]

    right_half = ring_gather([right_chunk], z)[0]
    blocks = ring_gather(chunk, z)
    right_half, blocks = lax.optimization_barrier((right_half, blocks))
    right_other = cross(right_half)
    right_all = jnp.where(
        first,
        jnp.concatenate([right_half, right_other], 1),
        jnp.concatenate([right_other, right_half], 1),
    )
    right_all = right_all.reshape(SIDES, RING, cols, width).transpose(1, 0, 2, 3)
    right_all = right_all.reshape(RING * SIDES * cols, width)

    rotated = jnp.einsum(
        "bkr,bck->brc", blocks, both, preferred_element_type=jnp.float32
    ).astype(jnp.bfloat16)
    values = ring_all_to_all(rotated.reshape(RING, row_part, 2 * SIDES * cols))
    second_new, returning = right_stage(values, right_all, second[0])
    values = ring_all_to_all(returning).reshape(count, BLK, SIDES * cols)
    devices = lax.axis_size("shard") * lax.axis_size("layer")
    raw_mine, raw_give, sums = raw_stage(values, blocks, devices)
    raw_other = cross(raw_give).astype(jnp.float32)
    total = jnp.sum(lax.all_to_all(sums, ("shard", "layer"), 0, 0))
    cells = lax.axis_size("layer") * grad.shape[0] * rows_all * cols * RING * SIDES
    factor = jnp.minimum(1.0, clip_limit / jnp.sqrt(total / cells + 1e-06))
    direction = jnp.where(
        first,
        jnp.concatenate([raw_mine, raw_other], 1),
        jnp.concatenate([raw_other, raw_mine], 1),
    )
    direction = (factor * direction).astype(jnp.bfloat16)
    return (moment_new.T[None], second_new[None], direction.T[None])


def solution(mesh):
    placed = (
        P("layer", None, "shard"),
        P("layer", None, "shard"),
        P("layer", "shard", None),
        P("layer", "shard", None, None),
        P("layer", "shard", None, None),
        P("layer", None),
    )
    return jax.shard_map(
        body,
        mesh=mesh,
        in_specs=placed,
        out_specs=(P("layer", None, "shard"), P("layer", "shard", None), P("layer", None, "shard")),
        check_vma=False,
    )
```

```python
import functools

import jax
import jax.numpy as jnp
from jax import lax
from jax.experimental import pallas as pl
from jax.experimental.pallas import tpu as pltpu
from jax.sharding import PartitionSpec as P

BLK = 1152
RING = 8
SIDES = 2
COUNT = 2
TILE = 256

first_decay = 0.9
second_decay = 0.95
guard_eps = 1e-08
clip_limit = 0.2


def rings():
    return [[y * RING + z for z in range(RING)] for y in range(SIDES)]


def ring_shift(value, step):
    pairs = [(y * RING + z, y * RING + (z + step) % RING) for y in range(SIDES) for z in range(RING)]
    return lax.ppermute(value, "shard", pairs)


def cross(value):
    return lax.ppermute(value, "shard", [(s, (s + RING) % (RING * SIDES)) for s in range(RING * SIDES)])


def ring_all_to_all(value):
    return lax.all_to_all(value, "shard", 0, 0, axis_index_groups=rings())


def ring_gather(chunks, z):
    rows = chunks[0].shape[0]
    whole = unset((len(chunks), RING * rows) + chunks[0].shape[1:], chunks[0].dtype)

    def put(whole, piece, i, place):
        return lax.dynamic_update_slice(whole, piece[None], (i, ((place + RING) % RING) * rows, 0))

    forward = list(chunks)
    backward = list(chunks)
    for i, chunk in enumerate(chunks):
        whole = put(whole, chunk, i, z)
    for step in range(1, RING // 2):
        for i in range(len(chunks)):
            forward[i] = ring_shift(forward[i], 1)
            backward[i] = ring_shift(backward[i], -1)
            whole = put(whole, forward[i], i, z - step)
            whole = put(whole, backward[i], i, z + step)
    for i in range(len(chunks)):
        far = ring_shift(forward[i], 1) if i % 2 == 0 else ring_shift(backward[i], -1)
        whole = put(whole, far, i, z + RING // 2)
    return whole


def unset(shape, dtype):
    return pl.pallas_call(
        lambda out: None,
        out_shape=jax.ShapeDtypeStruct(shape, dtype),
        out_specs=pl.BlockSpec(memory_space=pl.ANY),
    )()


def after(values, ready):
    count = len(values)
    return pl.pallas_call(
        lambda *refs: None,
        out_shape=[jax.ShapeDtypeStruct(value.shape, value.dtype) for value in values],
        in_specs=[pl.BlockSpec(memory_space=pl.ANY)] * (count + len(ready)),
        out_specs=[pl.BlockSpec(memory_space=pl.ANY)] * count,
        input_output_aliases={i: i for i in range(count)},
    )(*values, *ready)


def cut_kernel(owners, left, right, *pieces):
    me = lax.axis_index("shard")
    z = lax.rem(me, RING)
    holds_right = owners[0, owners.shape[1] // 4] == me
    rows, lanes = right.shape[1:]

    @pl.when(holds_right)
    def _():
        for step, piece in enumerate(pieces):
            piece[:rows, :lanes] = right[lax.rem(z + step, RING)]

    @pl.when(jnp.logical_not(holds_right))
    def _():
        for step, piece in enumerate(pieces):
            piece[...] = left[lax.rem(z + step, RING)]


def cut_slot(owners, left, right):
    return pl.pallas_call(
        cut_kernel,
        out_shape=[jax.ShapeDtypeStruct(left.shape[1:], left.dtype)] * RING,
        in_specs=[
            pl.BlockSpec(memory_space=pltpu.SMEM),
            pl.BlockSpec(memory_space=pltpu.VMEM),
            pl.BlockSpec(memory_space=pltpu.VMEM),
        ],
        compiler_params=pltpu.CompilerParams(vmem_limit_bytes=24 * 1024 * 1024),
    )(owners, left, right)


def raw_kernel(values, blocks, mine, other, sums):
    y = lax.div(lax.axis_index("shard"), RING)
    cols, order = mine.shape[1:]
    step = order // 3
    total = jnp.zeros((1, 128), jnp.float32)
    for i in range(COUNT):
        back = values[i].T
        for j in range(3):
            lanes = slice(j * step, (j + 1) * step)
            raw = lax.dot_general(
                back, blocks[i, lanes, :], (((1,), (1,)), ((), ())), preferred_element_type=jnp.float32
            )
            low = raw[:cols]
            high = raw[cols:]
            mine[i, :, lanes] = jnp.where(y == 0, low, high)
            other[i, :, lanes] = jnp.where(y == 0, high, low).astype(jnp.bfloat16)
            squares = jnp.sum(raw * raw, 0, keepdims=True)
            for k in range(step // 128):
                total += squares[:, k * 128 : (k + 1) * 128]
    sums[...] = jnp.broadcast_to(total, sums.shape)


def raw_stage(values, blocks, devices):
    count, order, pairs = values.shape
    cols = pairs // SIDES
    return pl.pallas_call(
        raw_kernel,
        out_shape=(
            jax.ShapeDtypeStruct((count, cols, order), jnp.float32),
            jax.ShapeDtypeStruct((count, cols, order), jnp.bfloat16),
            jax.ShapeDtypeStruct((devices, 128), jnp.float32),
        ),
        compiler_params=pltpu.CompilerParams(vmem_limit_bytes=24 * 1024 * 1024),
    )(values, blocks)


def clip_kernel(cells, sums, mine, other, out):
    y = lax.div(lax.axis_index("shard"), RING)
    count, _, order = mine.shape
    total = jnp.sum(jnp.sum(sums[...], 0, keepdims=True), 1, keepdims=True)
    factor = jnp.minimum(1.0, clip_limit / jnp.sqrt(total / cells + 1e-06))
    for i in range(count):
        own = factor * mine[i]
        far = factor * other[i].astype(jnp.float32)
        low = slice(i * order, (i + 1) * order)
        high = slice((count + i) * order, (count + i + 1) * order)
        out[:, low] = jnp.where(y == 0, own, far).astype(jnp.bfloat16)
        out[:, high] = jnp.where(y == 0, far, own).astype(jnp.bfloat16)


def clip_stage(sums, mine, other, cells):
    count, cols, order = mine.shape
    return pl.pallas_call(
        functools.partial(clip_kernel, cells),
        out_shape=jax.ShapeDtypeStruct((cols, SIDES * count * order), jnp.bfloat16),
        compiler_params=pltpu.CompilerParams(vmem_limit_bytes=24 * 1024 * 1024),
    )(sums, mine, other)


def right_kernel(values, right, second, second_out, out, scaled):
    rows = second.shape[0]
    pair = out.shape[2]
    places = values.shape[0]
    grad_left = jnp.concatenate([values[i, :, :pair] for i in range(places)], 1)
    moment_left = jnp.concatenate([values[i, :, pair:] for i in range(places)], 1)

    def turn(j, carry):
        lanes = pl.ds(pl.multiple_of(j * TILE, TILE), TILE)
        basis = right[:, lanes]
        grad_rot = jnp.dot(grad_left, basis, preferred_element_type=jnp.float32)
        moment_rot = jnp.dot(moment_left, basis, preferred_element_type=jnp.float32)
        second_new = second_decay * second[:, lanes] + (1.0 - second_decay) * grad_rot * grad_rot
        second_out[:, lanes] = second_new
        scaled[:, lanes] = (moment_rot / (jnp.sqrt(second_new) + guard_eps)).astype(jnp.bfloat16)
        return carry

    lax.fori_loop(0, second.shape[1] // TILE, turn, 0)

    def turn_back(j, carry):
        basis = right[pl.ds(pl.multiple_of(j * TILE, TILE), TILE), :]
        back = lax.dot_general(
            scaled[...], basis, (((1,), (1,)), ((), ())), preferred_element_type=jnp.float32
        ).astype(jnp.bfloat16)
        for i in range(TILE // pair):
            out[j * (TILE // pair) + i] = back[:, i * pair : (i + 1) * pair]
        return carry

    lax.fori_loop(0, right.shape[0] // TILE, turn_back, 0)


def right_stage(values, right, second):
    places, rows, pairs = values.shape
    return pl.pallas_call(
        right_kernel,
        out_shape=(
            jax.ShapeDtypeStruct(second.shape, jnp.float32),
            jax.ShapeDtypeStruct((places, rows, pairs // 2), jnp.bfloat16),
        ),
        scratch_shapes=[pltpu.VMEM(second.shape, jnp.bfloat16)],
        compiler_params=pltpu.CompilerParams(vmem_limit_bytes=24 * 1024 * 1024),
    )(values, right, second)


def body(grad, momentum, second, left_slots, right_slots, owners):
    me = lax.axis_index("shard")
    y = me // RING
    z = me % RING
    rows_all = grad.shape[1]
    cols = grad.shape[2]
    half = rows_all // SIDES
    row_part = rows_all // (RING * SIDES)
    count = half // BLK
    width = right_slots.shape[-1]
    piece = BLK // RING
    own = owners[0]
    own_y = own // RING
    own_z = own % RING
    first = y == 0

    pieces = cut_slot(
        owners,
        left_slots[0, 0].reshape(RING, piece, BLK),
        right_slots[0, 0].reshape(RING, SIDES * cols, width),
    )
    eighths = unset((RING, piece, BLK), jnp.bfloat16)
    for step in (0, 4, 3, 5, 2, 6, 1, 7):
        part = pieces[step]
        if step:
            part = ring_shift(part, step)
        eighths = lax.dynamic_update_slice(eighths, part[None], ((z - step + RING) % RING, 0, 0))

    grad_t = grad[0].T
    moment_new = first_decay * momentum[0].T + (1.0 - first_decay) * grad_t.astype(jnp.float32)
    paired = jnp.stack([grad_t, moment_new.astype(jnp.bfloat16)])
    mine = lax.dynamic_slice_in_dim(paired, y * half, half, 2)
    other = cross(lax.dynamic_slice_in_dim(paired, (1 - y) * half, half, 2))
    eighths, other = lax.optimization_barrier((eighths, other))
    both = jnp.where(
        first, jnp.concatenate([mine, other], 1), jnp.concatenate([other, mine], 1)
    ).reshape(2 * SIDES * cols, half)
    both = jnp.stack([both[:, i * BLK : (i + 1) * BLK] for i in range(count)])

    def pick(block):
        return lax.dynamic_index_in_dim(eighths, own_z[block], 0, keepdims=False)

    side = width // SIDES
    keep_right = pick(SIDES * count)[: SIDES * cols, :width]
    give_right = lax.dynamic_slice_in_dim(keep_right, (1 - y) * side, side, 1)
    keep_right = lax.dynamic_slice_in_dim(keep_right, y * side, side, 1)
    took_right = cross(give_right)
    right_chunk = jnp.where(own_y[SIDES * count] == y, keep_right, took_right)
    give = [pick((1 - y) * count + i) for i in range(count)]
    give = after(give, [took_right])
    took = [cross(value) for value in give]
    chunk = [
        jnp.where(own_y[y * count + i] == y, pick(y * count + i), took[i]) for i in range(count)
    ]

    right_half = ring_gather([right_chunk], z)[0]
    blocks = ring_gather(chunk, z)
    right_other = cross(right_half)
    (both,) = after([both], [right_other])
    right_all = jnp.where(
        first,
        jnp.concatenate([right_half, right_other], 1),
        jnp.concatenate([right_other, right_half], 1),
    )
    right_all = right_all.reshape(SIDES, RING, cols, width).transpose(1, 0, 2, 3)
    right_all = right_all.reshape(RING * SIDES * cols, width)

    rotated = jnp.einsum(
        "bkr,bck->brc", blocks, both, preferred_element_type=jnp.float32
    ).astype(jnp.bfloat16)
    values = ring_all_to_all(rotated.reshape(RING, row_part, 2 * SIDES * cols))
    second_new, returning = right_stage(values, right_all, second[0])
    values = ring_all_to_all(returning).reshape(count, BLK, SIDES * cols)
    devices = lax.axis_size("shard") * lax.axis_size("layer")
    raw_mine, raw_give, sums = raw_stage(values, blocks, devices)
    raw_other = cross(raw_give)
    sums = lax.all_to_all(sums, ("shard", "layer"), 0, 0)
    cells = lax.axis_size("layer") * grad.shape[0] * rows_all * cols * RING * SIDES
    direction = clip_stage(sums, raw_mine, raw_other, float(cells))
    return (moment_new.T[None], second_new[None], direction.T[None])


def solution(mesh):
    placed = (
        P("layer", None, "shard"),
        P("layer", None, "shard"),
        P("layer", "shard", None),
        P("layer", "shard", None, None),
        P("layer", "shard", None, None),
        P("layer", None),
    )
    return jax.shard_map(
        body,
        mesh=mesh,
        in_specs=placed,
        out_specs=(P("layer", None, "shard"), P("layer", "shard", None), P("layer", None, "shard")),
        check_vma=False,
    )
```

```python
import functools

import jax
import jax.numpy as jnp
from jax import lax
from jax.experimental import pallas as pl
from jax.experimental.pallas import tpu as pltpu
from jax.sharding import PartitionSpec as P

BLK = 1152
RING = 8
SIDES = 2
COUNT = 2
TILE = 256

first_decay = 0.9
second_decay = 0.95
guard_eps = 1e-08
clip_limit = 0.2


def rings():
    return [[y * RING + z for z in range(RING)] for y in range(SIDES)]


def ring_shift(value, step):
    pairs = [(y * RING + z, y * RING + (z + step) % RING) for y in range(SIDES) for z in range(RING)]
    return lax.ppermute(value, "shard", pairs)


def cross(value):
    return lax.ppermute(value, "shard", [(s, (s + RING) % (RING * SIDES)) for s in range(RING * SIDES)])


def ring_all_to_all(value):
    return lax.all_to_all(value, "shard", 0, 0, axis_index_groups=rings())


def ring_gather(chunks, z):
    rows = chunks[0].shape[0]
    whole = unset((len(chunks), RING * rows) + chunks[0].shape[1:], chunks[0].dtype)

    def put(whole, piece, i, place):
        return lax.dynamic_update_slice(whole, piece[None], (i, ((place + RING) % RING) * rows, 0))

    forward = list(chunks)
    backward = list(chunks)
    for i, chunk in enumerate(chunks):
        whole = put(whole, chunk, i, z)
    for step in range(1, RING // 2):
        for i in range(len(chunks)):
            forward[i] = ring_shift(forward[i], 1)
            backward[i] = ring_shift(backward[i], -1)
            whole = put(whole, forward[i], i, z - step)
            whole = put(whole, backward[i], i, z + step)
    for i in range(len(chunks)):
        far = ring_shift(forward[i], 1) if i % 2 == 0 else ring_shift(backward[i], -1)
        whole = put(whole, far, i, z + RING // 2)
    return whole


def unset(shape, dtype):
    return pl.pallas_call(
        lambda out: None,
        out_shape=jax.ShapeDtypeStruct(shape, dtype),
        out_specs=pl.BlockSpec(memory_space=pltpu.VMEM),
        compiler_params=pltpu.CompilerParams(vmem_limit_bytes=8 * 1024 * 1024),
    )()


def after(values, ready):
    count = len(values)
    return pl.pallas_call(
        lambda *refs: None,
        out_shape=[jax.ShapeDtypeStruct(value.shape, value.dtype) for value in values],
        in_specs=[pl.BlockSpec(memory_space=pl.ANY)] * (count + len(ready)),
        out_specs=[pl.BlockSpec(memory_space=pl.ANY)] * count,
        input_output_aliases={i: i for i in range(count)},
    )(*values, *ready)


def cut_kernel(owners, left, right, *pieces):
    me = lax.axis_index("shard")
    z = lax.rem(me, RING)
    holds_right = owners[0, owners.shape[1] // 4] == me
    rows, lanes = right.shape[1:]

    @pl.when(holds_right)
    def _():
        for step, piece in enumerate(pieces):
            piece[:rows, :lanes] = right[lax.rem(z + step, RING)]

    @pl.when(jnp.logical_not(holds_right))
    def _():
        for step, piece in enumerate(pieces):
            piece[...] = left[lax.rem(z + step, RING)]


def cut_slot(owners, left, right):
    return pl.pallas_call(
        cut_kernel,
        out_shape=[jax.ShapeDtypeStruct(left.shape[1:], left.dtype)] * RING,
        in_specs=[
            pl.BlockSpec(memory_space=pltpu.SMEM),
            pl.BlockSpec(memory_space=pltpu.VMEM),
            pl.BlockSpec(memory_space=pltpu.VMEM),
        ],
        compiler_params=pltpu.CompilerParams(vmem_limit_bytes=24 * 1024 * 1024),
    )(owners, left, right)


def raw_kernel(values, blocks, mine, other, sums):
    y = lax.div(lax.axis_index("shard"), RING)
    cols, order = mine.shape[1:]
    step = order // 3
    total = jnp.zeros((1, 128), jnp.float32)
    for i in range(COUNT):
        back = values[i].T
        for j in range(3):
            lanes = slice(j * step, (j + 1) * step)
            raw = lax.dot_general(
                back, blocks[i, lanes, :], (((1,), (1,)), ((), ())), preferred_element_type=jnp.float32
            )
            low = raw[:cols]
            high = raw[cols:]
            mine[i, :, lanes] = jnp.where(y == 0, low, high)
            other[i, :, lanes] = jnp.where(y == 0, high, low).astype(jnp.bfloat16)
            squares = jnp.sum(raw * raw, 0, keepdims=True)
            for k in range(step // 128):
                total += squares[:, k * 128 : (k + 1) * 128]
    sums[...] = jnp.broadcast_to(total, sums.shape)


def raw_stage(values, blocks, devices):
    count, order, pairs = values.shape
    cols = pairs // SIDES
    return pl.pallas_call(
        raw_kernel,
        out_shape=(
            jax.ShapeDtypeStruct((count, cols, order), jnp.float32),
            jax.ShapeDtypeStruct((count, cols, order), jnp.bfloat16),
            jax.ShapeDtypeStruct((devices, 128), jnp.float32),
        ),
        compiler_params=pltpu.CompilerParams(vmem_limit_bytes=24 * 1024 * 1024),
    )(values, blocks)


def clip_kernel(cells, sums, mine, other, out):
    y = lax.div(lax.axis_index("shard"), RING)
    count, _, order = mine.shape
    total = jnp.sum(jnp.sum(sums[...], 0, keepdims=True), 1, keepdims=True)
    factor = jnp.minimum(1.0, clip_limit / jnp.sqrt(total / cells + 1e-06))
    for i in range(count):
        own = factor * mine[i]
        far = factor * other[i].astype(jnp.float32)
        low = slice(i * order, (i + 1) * order)
        high = slice((count + i) * order, (count + i + 1) * order)
        out[:, low] = jnp.where(y == 0, own, far).astype(jnp.bfloat16)
        out[:, high] = jnp.where(y == 0, far, own).astype(jnp.bfloat16)


def clip_stage(sums, mine, other, cells):
    count, cols, order = mine.shape
    return pl.pallas_call(
        functools.partial(clip_kernel, cells),
        out_shape=jax.ShapeDtypeStruct((cols, SIDES * count * order), jnp.bfloat16),
        compiler_params=pltpu.CompilerParams(vmem_limit_bytes=24 * 1024 * 1024),
    )(sums, mine, other)


def right_kernel(values, right, second, second_out, out, scaled):
    rows = second.shape[0]
    pair = out.shape[2]
    places = values.shape[0]
    grad_left = jnp.concatenate([values[i, :, :pair] for i in range(places)], 1)
    moment_left = jnp.concatenate([values[i, :, pair:] for i in range(places)], 1)

    def turn(j, carry):
        lanes = pl.ds(pl.multiple_of(j * TILE, TILE), TILE)
        basis = right[:, lanes]
        grad_rot = jnp.dot(grad_left, basis, preferred_element_type=jnp.float32)
        moment_rot = jnp.dot(moment_left, basis, preferred_element_type=jnp.float32)
        second_new = second_decay * second[:, lanes] + (1.0 - second_decay) * grad_rot * grad_rot
        second_out[:, lanes] = second_new
        scaled[:, lanes] = (moment_rot / (jnp.sqrt(second_new) + guard_eps)).astype(jnp.bfloat16)
        return carry

    lax.fori_loop(0, second.shape[1] // TILE, turn, 0)

    def turn_back(j, carry):
        basis = right[pl.ds(pl.multiple_of(j * TILE, TILE), TILE), :]
        back = lax.dot_general(
            scaled[...], basis, (((1,), (1,)), ((), ())), preferred_element_type=jnp.float32
        ).astype(jnp.bfloat16)
        for i in range(TILE // pair):
            out[j * (TILE // pair) + i] = back[:, i * pair : (i + 1) * pair]
        return carry

    lax.fori_loop(0, right.shape[0] // TILE, turn_back, 0)


def right_stage(values, right, second):
    places, rows, pairs = values.shape
    return pl.pallas_call(
        right_kernel,
        out_shape=(
            jax.ShapeDtypeStruct(second.shape, jnp.float32),
            jax.ShapeDtypeStruct((places, rows, pairs // 2), jnp.bfloat16),
        ),
        scratch_shapes=[pltpu.VMEM(second.shape, jnp.bfloat16)],
        compiler_params=pltpu.CompilerParams(vmem_limit_bytes=24 * 1024 * 1024),
    )(values, right, second)


def body(grad, momentum, second, left_slots, right_slots, owners):
    me = lax.axis_index("shard")
    y = me // RING
    z = me % RING
    rows_all = grad.shape[1]
    cols = grad.shape[2]
    half = rows_all // SIDES
    row_part = rows_all // (RING * SIDES)
    count = half // BLK
    width = right_slots.shape[-1]
    piece = BLK // RING
    own = owners[0]
    own_y = own // RING
    own_z = own % RING
    first = y == 0

    pieces = cut_slot(
        owners,
        left_slots[0, 0].reshape(RING, piece, BLK),
        right_slots[0, 0].reshape(RING, SIDES * cols, width),
    )
    eighths = unset((RING, piece, BLK), jnp.bfloat16)
    for step in (0, 1, 7, 4, 3, 5, 2, 6):
        part = pieces[step]
        if step:
            part = ring_shift(part, step)
        eighths = lax.dynamic_update_slice(eighths, part[None], ((z - step + RING) % RING, 0, 0))

    grad_t = grad[0].T
    moment_new = first_decay * momentum[0].T + (1.0 - first_decay) * grad_t.astype(jnp.float32)
    paired = jnp.stack([grad_t, moment_new.astype(jnp.bfloat16)])
    mine = lax.dynamic_slice_in_dim(paired, y * half, half, 2)
    other = cross(lax.dynamic_slice_in_dim(paired, (1 - y) * half, half, 2))
    eighths, other = lax.optimization_barrier((eighths, other))
    both = jnp.where(
        first, jnp.concatenate([mine, other], 1), jnp.concatenate([other, mine], 1)
    ).reshape(2 * SIDES * cols, half)
    both = jnp.stack([both[:, i * BLK : (i + 1) * BLK] for i in range(count)])

    def pick(block):
        return lax.dynamic_index_in_dim(eighths, own_z[block], 0, keepdims=False)

    side = width // SIDES
    keep_right = pick(SIDES * count)[: SIDES * cols, :width]
    give_right = lax.dynamic_slice_in_dim(keep_right, (1 - y) * side, side, 1)
    keep_right = lax.dynamic_slice_in_dim(keep_right, y * side, side, 1)
    took_right = cross(give_right)
    right_chunk = jnp.where(own_y[SIDES * count] == y, keep_right, took_right)
    give = [pick((1 - y) * count + i) for i in range(count)]
    give = after(give, [took_right])
    took = [cross(value) for value in give]
    chunk = [
        jnp.where(own_y[y * count + i] == y, pick(y * count + i), took[i]) for i in range(count)
    ]

    right_half = ring_gather([right_chunk], z)[0]
    blocks = ring_gather(chunk, z)
    right_other = cross(right_half)
    both, right_other = lax.optimization_barrier((both, right_other))
    right_all = jnp.where(
        first,
        jnp.concatenate([right_half, right_other], 1),
        jnp.concatenate([right_other, right_half], 1),
    )
    right_all = right_all.reshape(SIDES, RING, cols, width).transpose(1, 0, 2, 3)
    right_all = right_all.reshape(RING * SIDES * cols, width)

    rotated = jnp.einsum(
        "bkr,bck->brc", blocks, both, preferred_element_type=jnp.float32
    ).astype(jnp.bfloat16)
    values = ring_all_to_all(rotated.reshape(RING, row_part, 2 * SIDES * cols))
    second_new, returning = right_stage(values, right_all, second[0])
    values = ring_all_to_all(returning).reshape(count, BLK, SIDES * cols)
    devices = lax.axis_size("shard") * lax.axis_size("layer")
    raw_mine, raw_give, sums = raw_stage(values, blocks, devices)
    raw_other = cross(raw_give)
    sums = lax.all_to_all(sums, ("shard", "layer"), 0, 0)
    cells = lax.axis_size("layer") * grad.shape[0] * rows_all * cols * RING * SIDES
    direction = clip_stage(sums, raw_mine, raw_other, float(cells))
    return (moment_new.T[None], second_new[None], direction.T[None])


def solution(mesh):
    placed = (
        P("layer", None, "shard"),
        P("layer", None, "shard"),
        P("layer", "shard", None),
        P("layer", "shard", None, None),
        P("layer", "shard", None, None),
        P("layer", None),
    )
    return jax.shard_map(
        body,
        mesh=mesh,
        in_specs=placed,
        out_specs=(P("layer", None, "shard"), P("layer", "shard", None), P("layer", None, "shard")),
        check_vma=False,
    )
```

```python
import functools

import jax
import jax.numpy as jnp
from jax import lax
from jax.experimental import pallas as pl
from jax.experimental.pallas import tpu as pltpu
from jax.sharding import PartitionSpec as P

BLK = 1152
RING = 8
SIDES = 2
COUNT = 2
TILE = 256

first_decay = 0.9
second_decay = 0.95
guard_eps = 1e-08
clip_limit = 0.2


def rings():
    return [[y * RING + z for z in range(RING)] for y in range(SIDES)]


def ring_shift(value, step):
    pairs = [(y * RING + z, y * RING + (z + step) % RING) for y in range(SIDES) for z in range(RING)]
    return lax.ppermute(value, "shard", pairs)


def cross(value):
    return lax.ppermute(value, "shard", [(s, (s + RING) % (RING * SIDES)) for s in range(RING * SIDES)])


def ring_all_to_all(value):
    return lax.all_to_all(value, "shard", 0, 0, axis_index_groups=rings())


def ring_gather(chunks, z):
    rows = chunks[0].shape[0]
    whole = unset((len(chunks), RING * rows) + chunks[0].shape[1:], chunks[0].dtype)

    def put(whole, piece, i, place):
        return lax.dynamic_update_slice(whole, piece[None], (i, ((place + RING) % RING) * rows, 0))

    forward = list(chunks)
    backward = list(chunks)
    for i, chunk in enumerate(chunks):
        whole = put(whole, chunk, i, z)
    for step in range(1, RING // 2):
        for i in range(len(chunks)):
            forward[i] = ring_shift(forward[i], 1)
            backward[i] = ring_shift(backward[i], -1)
            whole = put(whole, forward[i], i, z - step)
            whole = put(whole, backward[i], i, z + step)
    for i in range(len(chunks)):
        far = ring_shift(forward[i], 1) if i % 2 == 0 else ring_shift(backward[i], -1)
        whole = put(whole, far, i, z + RING // 2)
    return whole


def unset(shape, dtype):
    return pl.pallas_call(
        lambda out: None,
        out_shape=jax.ShapeDtypeStruct(shape, dtype),
        out_specs=pl.BlockSpec(memory_space=pltpu.VMEM),
        compiler_params=pltpu.CompilerParams(vmem_limit_bytes=8 * 1024 * 1024),
    )()


def cut_kernel(owners, left, right, *pieces):
    me = lax.axis_index("shard")
    z = lax.rem(me, RING)
    holds_right = owners[0, owners.shape[1] // 4] == me
    rows, lanes = right.shape[1:]

    @pl.when(holds_right)
    def _():
        for step, piece in enumerate(pieces):
            piece[:rows, :lanes] = right[lax.rem(z + step, RING)]

    @pl.when(jnp.logical_not(holds_right))
    def _():
        for step, piece in enumerate(pieces):
            piece[...] = left[lax.rem(z + step, RING)]


def cut_slot(owners, left, right):
    return pl.pallas_call(
        cut_kernel,
        out_shape=[jax.ShapeDtypeStruct(left.shape[1:], left.dtype)] * RING,
        in_specs=[
            pl.BlockSpec(memory_space=pltpu.SMEM),
            pl.BlockSpec(memory_space=pltpu.VMEM),
            pl.BlockSpec(memory_space=pltpu.VMEM),
        ],
        compiler_params=pltpu.CompilerParams(vmem_limit_bytes=24 * 1024 * 1024),
    )(owners, left, right)


def raw_kernel(values, blocks, mine, other, sums):
    y = lax.div(lax.axis_index("shard"), RING)
    cols, order = mine.shape[1:]
    step = order // 3
    total = jnp.zeros((1, 128), jnp.float32)
    for i in range(COUNT):
        back = values[i].T
        for j in range(3):
            lanes = slice(j * step, (j + 1) * step)
            raw = lax.dot_general(
                back, blocks[i, lanes, :], (((1,), (1,)), ((), ())), preferred_element_type=jnp.float32
            )
            low = raw[:cols]
            high = raw[cols:]
            mine[i, :, lanes] = jnp.where(y == 0, low, high)
            other[i, :, lanes] = jnp.where(y == 0, high, low).astype(jnp.bfloat16)
            squares = jnp.sum(raw * raw, 0, keepdims=True)
            for k in range(step // 128):
                total += squares[:, k * 128 : (k + 1) * 128]
    sums[...] = jnp.broadcast_to(total, sums.shape)


def raw_stage(values, blocks, devices):
    count, order, pairs = values.shape
    cols = pairs // SIDES
    return pl.pallas_call(
        raw_kernel,
        out_shape=(
            jax.ShapeDtypeStruct((count, cols, order), jnp.float32),
            jax.ShapeDtypeStruct((count, cols, order), jnp.bfloat16),
            jax.ShapeDtypeStruct((devices, 128), jnp.float32),
        ),
        compiler_params=pltpu.CompilerParams(vmem_limit_bytes=24 * 1024 * 1024),
    )(values, blocks)


def clip_kernel(cells, sums, mine, other, out):
    y = lax.div(lax.axis_index("shard"), RING)
    count, _, order = mine.shape
    total = jnp.sum(jnp.sum(sums[...], 0, keepdims=True), 1, keepdims=True)
    factor = jnp.minimum(1.0, clip_limit / jnp.sqrt(total / cells + 1e-06))
    for i in range(count):
        own = factor * mine[i]
        far = factor * other[i].astype(jnp.float32)
        low = slice(i * order, (i + 1) * order)
        high = slice((count + i) * order, (count + i + 1) * order)
        out[:, low] = jnp.where(y == 0, own, far).astype(jnp.bfloat16)
        out[:, high] = jnp.where(y == 0, far, own).astype(jnp.bfloat16)


def clip_stage(sums, mine, other, cells):
    count, cols, order = mine.shape
    return pl.pallas_call(
        functools.partial(clip_kernel, cells),
        out_shape=jax.ShapeDtypeStruct((cols, SIDES * count * order), jnp.bfloat16),
        compiler_params=pltpu.CompilerParams(vmem_limit_bytes=24 * 1024 * 1024),
    )(sums, mine, other)


def right_kernel(values, right, second, second_out, out, scaled):
    rows = second.shape[0]
    pair = out.shape[2]
    places = values.shape[0]
    grad_left = jnp.concatenate([values[i, :, :pair] for i in range(places)], 1)
    moment_left = jnp.concatenate([values[i, :, pair:] for i in range(places)], 1)

    def turn(j, carry):
        lanes = pl.ds(pl.multiple_of(j * TILE, TILE), TILE)
        basis = right[:, lanes]
        grad_rot = jnp.dot(grad_left, basis, preferred_element_type=jnp.float32)
        moment_rot = jnp.dot(moment_left, basis, preferred_element_type=jnp.float32)
        second_new = second_decay * second[:, lanes] + (1.0 - second_decay) * grad_rot * grad_rot
        second_out[:, lanes] = second_new
        scaled[:, lanes] = (moment_rot / (jnp.sqrt(second_new) + guard_eps)).astype(jnp.bfloat16)
        return carry

    lax.fori_loop(0, second.shape[1] // TILE, turn, 0)

    def turn_back(j, carry):
        basis = right[pl.ds(pl.multiple_of(j * TILE, TILE), TILE), :]
        back = lax.dot_general(
            scaled[...], basis, (((1,), (1,)), ((), ())), preferred_element_type=jnp.float32
        ).astype(jnp.bfloat16)
        for i in range(TILE // pair):
            out[j * (TILE // pair) + i] = back[:, i * pair : (i + 1) * pair]
        return carry

    lax.fori_loop(0, right.shape[0] // TILE, turn_back, 0)


def right_stage(values, right, second):
    places, rows, pairs = values.shape
    return pl.pallas_call(
        right_kernel,
        out_shape=(
            jax.ShapeDtypeStruct(second.shape, jnp.float32),
            jax.ShapeDtypeStruct((places, rows, pairs // 2), jnp.bfloat16),
        ),
        scratch_shapes=[pltpu.VMEM(second.shape, jnp.bfloat16)],
        compiler_params=pltpu.CompilerParams(vmem_limit_bytes=24 * 1024 * 1024),
    )(values, right, second)


def body(grad, momentum, second, left_slots, right_slots, owners):
    me = lax.axis_index("shard")
    y = me // RING
    z = me % RING
    rows_all = grad.shape[1]
    cols = grad.shape[2]
    half = rows_all // SIDES
    row_part = rows_all // (RING * SIDES)
    count = half // BLK
    width = right_slots.shape[-1]
    piece = BLK // RING
    own = owners[0]
    own_y = own // RING
    own_z = own % RING
    first = y == 0

    pieces = cut_slot(
        owners,
        left_slots[0, 0].reshape(RING, piece, BLK),
        right_slots[0, 0].reshape(RING, SIDES * cols, width),
    )
    eighths = unset((RING, piece, BLK), jnp.bfloat16)
    for step in (0, 1, 7, 4, 3, 5, 2, 6):
        part = pieces[step]
        if step:
            part = ring_shift(part, step)
        eighths = lax.dynamic_update_slice(eighths, part[None], ((z - step + RING) % RING, 0, 0))

    grad_t = grad[0].T
    moment_new = first_decay * momentum[0].T + (1.0 - first_decay) * grad_t.astype(jnp.float32)
    paired = jnp.stack([grad_t, moment_new.astype(jnp.bfloat16)])
    mine = lax.dynamic_slice_in_dim(paired, y * half, half, 2)
    other = cross(lax.dynamic_slice_in_dim(paired, (1 - y) * half, half, 2))
    eighths, other = lax.optimization_barrier((eighths, other))
    both = jnp.where(
        first, jnp.concatenate([mine, other], 1), jnp.concatenate([other, mine], 1)
    ).reshape(2 * SIDES * cols, half)
    both = jnp.stack([both[:, i * BLK : (i + 1) * BLK] for i in range(count)])

    def pick(block):
        return lax.dynamic_index_in_dim(eighths, own_z[block], 0, keepdims=False)

    side = width // SIDES
    keep_right = pick(SIDES * count)[: SIDES * cols, :width]
    give_right = lax.dynamic_slice_in_dim(keep_right, (1 - y) * side, side, 1)
    keep_right = lax.dynamic_slice_in_dim(keep_right, y * side, side, 1)
    took_right = cross(give_right)
    right_chunk = jnp.where(own_y[SIDES * count] == y, keep_right, took_right)
    give = [pick((1 - y) * count + i) for i in range(count)]
    give, took_right = lax.optimization_barrier((give, took_right))
    took = [cross(value) for value in give]
    chunk = [
        jnp.where(own_y[y * count + i] == y, pick(y * count + i), took[i]) for i in range(count)
    ]

    right_half = ring_gather([right_chunk], z)[0]
    blocks = ring_gather(chunk, z)
    right_other = cross(right_half)
    both, right_other = lax.optimization_barrier((both, right_other))
    right_all = jnp.where(
        first,
        jnp.concatenate([right_half, right_other], 1),
        jnp.concatenate([right_other, right_half], 1),
    )
    right_all = right_all.reshape(SIDES, RING, cols, width).transpose(1, 0, 2, 3)
    right_all = right_all.reshape(RING * SIDES * cols, width)

    rotated = jnp.einsum(
        "bkr,bck->brc", blocks, both, preferred_element_type=jnp.float32
    ).astype(jnp.bfloat16)
    values = ring_all_to_all(rotated.reshape(RING, row_part, 2 * SIDES * cols))
    second_new, returning = right_stage(values, right_all, second[0])
    values = ring_all_to_all(returning).reshape(count, BLK, SIDES * cols)
    devices = lax.axis_size("shard") * lax.axis_size("layer")
    raw_mine, raw_give, sums = raw_stage(values, blocks, devices)
    raw_other = cross(raw_give)
    sums = lax.all_to_all(sums, ("shard", "layer"), 0, 0)
    cells = lax.axis_size("layer") * grad.shape[0] * rows_all * cols * RING * SIDES
    direction = clip_stage(sums, raw_mine, raw_other, float(cells))
    return (moment_new.T[None], second_new[None], direction.T[None])


def solution(mesh):
    placed = (
        P("layer", None, "shard"),
        P("layer", None, "shard"),
        P("layer", "shard", None),
        P("layer", "shard", None, None),
        P("layer", "shard", None, None),
        P("layer", None),
    )
    return jax.shard_map(
        body,
        mesh=mesh,
        in_specs=placed,
        out_specs=(P("layer", None, "shard"), P("layer", "shard", None), P("layer", None, "shard")),
        check_vma=False,
    )
```

```python
import functools

import jax
import jax.numpy as jnp
from jax import lax
from jax.experimental import pallas as pl
from jax.experimental.pallas import tpu as pltpu
from jax.sharding import PartitionSpec as P

BLK = 1152
RING = 8
SIDES = 2
COUNT = 2
TILE = 256

first_decay = 0.9
second_decay = 0.95
guard_eps = 1e-08
clip_limit = 0.2


def rings():
    return [[y * RING + z for z in range(RING)] for y in range(SIDES)]


def ring_shift(value, step):
    pairs = [(y * RING + z, y * RING + (z + step) % RING) for y in range(SIDES) for z in range(RING)]
    return lax.ppermute(value, "shard", pairs)


def cross(value):
    return lax.ppermute(value, "shard", [(s, (s + RING) % (RING * SIDES)) for s in range(RING * SIDES)])


def ring_all_to_all(value):
    return lax.all_to_all(value, "shard", 0, 0, axis_index_groups=rings())


def ring_gather(chunks, z):
    rows = chunks[0].shape[0]
    whole = unset((len(chunks), RING * rows) + chunks[0].shape[1:], chunks[0].dtype)

    def put(whole, piece, i, place):
        return lax.dynamic_update_slice(whole, piece[None], (i, ((place + RING) % RING) * rows, 0))

    forward = list(chunks)
    backward = list(chunks)
    for i, chunk in enumerate(chunks):
        whole = put(whole, chunk, i, z)
    for step in range(1, RING // 2):
        for i in range(len(chunks)):
            forward[i] = ring_shift(forward[i], 1)
            backward[i] = ring_shift(backward[i], -1)
            whole = put(whole, forward[i], i, z - step)
            whole = put(whole, backward[i], i, z + step)
    for i in range(len(chunks)):
        far = ring_shift(forward[i], 1) if i % 2 == 0 else ring_shift(backward[i], -1)
        whole = put(whole, far, i, z + RING // 2)
    return whole


def unset(shape, dtype):
    return pl.pallas_call(
        lambda out: None,
        out_shape=jax.ShapeDtypeStruct(shape, dtype),
        out_specs=pl.BlockSpec(memory_space=pltpu.VMEM),
        compiler_params=pltpu.CompilerParams(vmem_limit_bytes=8 * 1024 * 1024),
    )()


def cut_kernel(owners, left, right, *pieces):
    me = lax.axis_index("shard")
    z = lax.rem(me, RING)
    holds_right = owners[0, owners.shape[1] // 4] == me
    rows, lanes = right.shape[1:]

    @pl.when(holds_right)
    def _():
        for step, piece in enumerate(pieces):
            piece[:rows, :lanes] = right[lax.rem(z + step, RING)]

    @pl.when(jnp.logical_not(holds_right))
    def _():
        for step, piece in enumerate(pieces):
            piece[...] = left[lax.rem(z + step, RING)]


def cut_slot(owners, left, right):
    return pl.pallas_call(
        cut_kernel,
        out_shape=[jax.ShapeDtypeStruct(left.shape[1:], left.dtype)] * RING,
        in_specs=[
            pl.BlockSpec(memory_space=pltpu.SMEM),
            pl.BlockSpec(memory_space=pltpu.VMEM),
            pl.BlockSpec(memory_space=pltpu.VMEM),
        ],
        compiler_params=pltpu.CompilerParams(vmem_limit_bytes=24 * 1024 * 1024),
    )(owners, left, right)


def raw_kernel(i, values, blocks, before, mine, other, sums):
    y = lax.div(lax.axis_index("shard"), RING)
    cols, order = mine.shape
    step = order // 3
    total = before[...]
    back = values[i].T
    for j in range(3):
        lanes = slice(j * step, (j + 1) * step)
        raw = lax.dot_general(
            back, blocks[i, lanes, :], (((1,), (1,)), ((), ())), preferred_element_type=jnp.float32
        )
        low = raw[:cols]
        high = raw[cols:]
        mine[:, lanes] = jnp.where(y == 0, low, high)
        other[:, lanes] = jnp.where(y == 0, high, low).astype(jnp.bfloat16)
        squares = jnp.sum(raw * raw, 0, keepdims=True)
        for k in range(step // 128):
            total += squares[:, k * 128 : (k + 1) * 128]
    sums[...] = jnp.broadcast_to(total, sums.shape)


def raw_stage(i, values, blocks, before, copies):
    _, order, pairs = values.shape
    cols = pairs // SIDES
    return pl.pallas_call(
        functools.partial(raw_kernel, i),
        out_shape=(
            jax.ShapeDtypeStruct((cols, order), jnp.float32),
            jax.ShapeDtypeStruct((cols, order), jnp.bfloat16),
            jax.ShapeDtypeStruct((copies, 128), jnp.float32),
        ),
        compiler_params=pltpu.CompilerParams(vmem_limit_bytes=24 * 1024 * 1024),
    )(values, blocks, before)


def clip_kernel(cells, sums, *refs):
    mine = refs[:COUNT]
    other = refs[COUNT : 2 * COUNT]
    out = refs[2 * COUNT]
    y = lax.div(lax.axis_index("shard"), RING)
    order = mine[0].shape[1]
    total = jnp.sum(jnp.sum(sums[...], 0, keepdims=True), 1, keepdims=True)
    factor = jnp.minimum(1.0, clip_limit / jnp.sqrt(total / cells + 1e-06))
    for i in range(COUNT):
        own = factor * mine[i][...]
        far = factor * other[i][...].astype(jnp.float32)
        low = slice(i * order, (i + 1) * order)
        high = slice((COUNT + i) * order, (COUNT + i + 1) * order)
        out[:, low] = jnp.where(y == 0, own, far).astype(jnp.bfloat16)
        out[:, high] = jnp.where(y == 0, far, own).astype(jnp.bfloat16)


def clip_stage(sums, mine, other, cells):
    cols, order = mine[0].shape
    return pl.pallas_call(
        functools.partial(clip_kernel, cells),
        out_shape=jax.ShapeDtypeStruct((cols, SIDES * COUNT * order), jnp.bfloat16),
        compiler_params=pltpu.CompilerParams(vmem_limit_bytes=24 * 1024 * 1024),
    )(sums, *mine, *other)


def right_kernel(values, right, second, second_out, out, scaled):
    rows = second.shape[0]
    pair = out.shape[2]
    places = values.shape[0]
    grad_left = jnp.concatenate([values[i, :, :pair] for i in range(places)], 1)
    moment_left = jnp.concatenate([values[i, :, pair:] for i in range(places)], 1)

    def turn(j, carry):
        lanes = pl.ds(pl.multiple_of(j * TILE, TILE), TILE)
        basis = right[:, lanes]
        grad_rot = jnp.dot(grad_left, basis, preferred_element_type=jnp.float32)
        moment_rot = jnp.dot(moment_left, basis, preferred_element_type=jnp.float32)
        second_new = second_decay * second[:, lanes] + (1.0 - second_decay) * grad_rot * grad_rot
        second_out[:, lanes] = second_new
        scaled[:, lanes] = (moment_rot / (jnp.sqrt(second_new) + guard_eps)).astype(jnp.bfloat16)
        return carry

    lax.fori_loop(0, second.shape[1] // TILE, turn, 0)

    def turn_back(j, carry):
        basis = right[pl.ds(pl.multiple_of(j * TILE, TILE), TILE), :]
        back = lax.dot_general(
            scaled[...], basis, (((1,), (1,)), ((), ())), preferred_element_type=jnp.float32
        ).astype(jnp.bfloat16)
        for i in range(TILE // pair):
            out[j * (TILE // pair) + i] = back[:, i * pair : (i + 1) * pair]
        return carry

    lax.fori_loop(0, right.shape[0] // TILE, turn_back, 0)


def right_stage(values, right, second):
    places, rows, pairs = values.shape
    return pl.pallas_call(
        right_kernel,
        out_shape=(
            jax.ShapeDtypeStruct(second.shape, jnp.float32),
            jax.ShapeDtypeStruct((places, rows, pairs // 2), jnp.bfloat16),
        ),
        scratch_shapes=[pltpu.VMEM(second.shape, jnp.bfloat16)],
        compiler_params=pltpu.CompilerParams(vmem_limit_bytes=24 * 1024 * 1024),
    )(values, right, second)


def body(grad, momentum, second, left_slots, right_slots, owners):
    me = lax.axis_index("shard")
    y = me // RING
    z = me % RING
    rows_all = grad.shape[1]
    cols = grad.shape[2]
    half = rows_all // SIDES
    row_part = rows_all // (RING * SIDES)
    count = half // BLK
    width = right_slots.shape[-1]
    piece = BLK // RING
    own = owners[0]
    own_y = own // RING
    own_z = own % RING
    first = y == 0

    pieces = cut_slot(
        owners,
        left_slots[0, 0].reshape(RING, piece, BLK),
        right_slots[0, 0].reshape(RING, SIDES * cols, width),
    )
    eighths = unset((RING, piece, BLK), jnp.bfloat16)
    for step in (0, 1, 7, 4, 3, 5, 2, 6):
        part = pieces[step]
        if step:
            part = ring_shift(part, step)
        eighths = lax.dynamic_update_slice(eighths, part[None], ((z - step + RING) % RING, 0, 0))

    grad_t = grad[0].T
    moment_new = first_decay * momentum[0].T + (1.0 - first_decay) * grad_t.astype(jnp.float32)
    paired = jnp.stack([grad_t, moment_new.astype(jnp.bfloat16)])
    mine = lax.dynamic_slice_in_dim(paired, y * half, half, 2)
    other = cross(lax.dynamic_slice_in_dim(paired, (1 - y) * half, half, 2))
    eighths, other = lax.optimization_barrier((eighths, other))
    both = jnp.where(
        first, jnp.concatenate([mine, other], 1), jnp.concatenate([other, mine], 1)
    ).reshape(2 * SIDES * cols, half)
    both = jnp.stack([both[:, i * BLK : (i + 1) * BLK] for i in range(count)])

    def pick(block):
        return lax.dynamic_index_in_dim(eighths, own_z[block], 0, keepdims=False)

    side = width // SIDES
    keep_right = pick(SIDES * count)[: SIDES * cols, :width]
    give_right = lax.dynamic_slice_in_dim(keep_right, (1 - y) * side, side, 1)
    keep_right = lax.dynamic_slice_in_dim(keep_right, y * side, side, 1)
    took_right = cross(give_right)
    right_chunk = jnp.where(own_y[SIDES * count] == y, keep_right, took_right)
    give = [pick((1 - y) * count + i) for i in range(count)]
    give, took_right = lax.optimization_barrier((give, took_right))
    took = [cross(value) for value in give]
    chunk = [
        jnp.where(own_y[y * count + i] == y, pick(y * count + i), took[i]) for i in range(count)
    ]

    right_half = ring_gather([right_chunk], z)[0]
    blocks = ring_gather(chunk, z)
    right_other = cross(right_half)
    both, right_other = lax.optimization_barrier((both, right_other))
    right_all = jnp.where(
        first,
        jnp.concatenate([right_half, right_other], 1),
        jnp.concatenate([right_other, right_half], 1),
    )
    right_all = right_all.reshape(SIDES, RING, cols, width).transpose(1, 0, 2, 3)
    right_all = right_all.reshape(RING * SIDES * cols, width)

    rotated = jnp.einsum(
        "bkr,bck->brc", blocks, both, preferred_element_type=jnp.float32
    ).astype(jnp.bfloat16)
    values = ring_all_to_all(rotated.reshape(RING, row_part, 2 * SIDES * cols))
    second_new, returning = right_stage(values, right_all, second[0])
    values = ring_all_to_all(returning).reshape(count, BLK, SIDES * cols)
    devices = lax.axis_size("shard") * lax.axis_size("layer")
    raw_mine, raw_other = [], []
    sums = jnp.zeros((1, 128), jnp.float32)
    for i in range(count):
        raw, give, sums = raw_stage(i, values, blocks, sums, 1 if i < count - 1 else devices)
        raw_mine.append(raw)
        raw_other.append(cross(give))
    sums = lax.all_to_all(sums, ("shard", "layer"), 0, 0)
    cells = lax.axis_size("layer") * grad.shape[0] * rows_all * cols * RING * SIDES
    direction = clip_stage(sums, raw_mine, raw_other, float(cells))
    return (moment_new.T[None], second_new[None], direction.T[None])


def solution(mesh):
    placed = (
        P("layer", None, "shard"),
        P("layer", None, "shard"),
        P("layer", "shard", None),
        P("layer", "shard", None, None),
        P("layer", "shard", None, None),
        P("layer", None),
    )
    return jax.shard_map(
        body,
        mesh=mesh,
        in_specs=placed,
        out_specs=(P("layer", None, "shard"), P("layer", "shard", None), P("layer", None, "shard")),
        check_vma=False,
    )
```
